32 devices in a mesh: row: 4 (over y, core), col: 8 (over z, x).
Axes of the slice: x: 2, y: 2, z: 4, core: 2. Of those that a mesh axis runs over, the one named last changes fastest.
Arguments:
- x_paper: bfloat16 [8192, 768], P(('row', 'col')), may hold values from -6 to 6
- x_author: bfloat16 [8192, 768], P(('row', 'col')), may hold values from -6 to 6
- cite_nbr: int32 [8192, 16], P(('row', 'col')), may hold values from -1 to 2047, as said below
- write_src: int32 [32, 32, 4], P(('row', 'col')), may hold values from -1 to 255, as said below
- write_dst: int32 [32, 32, 4], P(('row', 'col')), may hold values from -1 to 255, as said below
- w_self_paper: bfloat16 [768, 1024], replicated, may hold values from -0.21875 to 0.21875
- w_cite: bfloat16 [768, 1024], replicated, may hold values from -0.21875 to 0.21875
- w_write: bfloat16 [768, 1024], replicated, may hold values from -0.21875 to 0.21875
- w_self_author: bfloat16 [768, 1024], replicated, may hold values from -0.21875 to 0.21875
- w_written: bfloat16 [768, 1024], replicated, may hold values from -0.21875 to 0.21875
- grad_paper: bfloat16 [8192, 1024], P(('row', 'col')), may hold values from -6 to 6
- grad_author: bfloat16 [8192, 1024], P(('row', 'col')), may hold values from -6 to 6
Outputs:
- out_paper: bfloat16 [8192, 1024], P(('row', 'col'))
- out_author: bfloat16 [8192, 1024], P(('row', 'col'))
- dx_paper: bfloat16 [8192, 768], P(('row', 'col'))
- dx_author: bfloat16 [8192, 768], P(('row', 'col'))
- dweights: float32 [5, 768, 1024], P(None, 'row', 'col')
The draws below stay inside these ranges and needn't reach their ends.
Inputs may be any that keep to these rules, and one draw needn't show every extreme that they name: `cite_nbr`: entries of a row that are -1 stand for no citation and come after all others; a value e >= 0 names the paper at position e of the paper's own block row. Some paper has all 16 entries. write_src[s, d, j] is -1 (empty slot) exactly where write_dst[d, s, j] is -1; otherwise it is an author position on device s. Some device d has every slot from every device s filled. write_dst[d, s, j] is -1 exactly where write_src[s, d, j] is -1; otherwise it is a paper position on device d. A paper may have several edges, also from one author.
All inputs are finite; a program needn't handle non-finite values.
Results may differ from the reference program's by a relative error of at most 0.0054.
Values may be sent and summed in bfloat16 or wider, within the bound.
A program may use at most 192 MiB of HBM per device.

```python
import jax
import jax.numpy as jnp
from jax import lax

D_IN = 768
D_OUT = 1024
P_DEV = 256
A_DEV = 256
CAP = 4
K_CITE = 16
PAPERS = 8192
AUTHORS = 8192
ROW_PAPERS = 2048
N_ROW = 4
DEVICES = 32


def write_common(key):
    keys = jax.random.split(key, 5)
    chance = jax.random.randint(keys[0], (DEVICES, 1, 1), 20, 96)
    roll = jax.random.randint(keys[1], (DEVICES, DEVICES, CAP), 0, 100)
    chosen = jax.random.randint(keys[2], (), 0, DEVICES)
    receiver = jnp.arange(DEVICES, dtype=jnp.int32)[:, None, None]
    sender = jnp.arange(DEVICES, dtype=jnp.int32)[None, :, None]
    position = jnp.arange(CAP, dtype=jnp.int32)[None, None, :]
    live = (roll < chance) | (receiver == chosen)
    corner = (receiver == chosen) & (sender == 0) & (position == 0)
    paper_pos = jax.random.randint(keys[3], (DEVICES, DEVICES, CAP), 0, P_DEV)
    author_pos = jax.random.randint(keys[4], (DEVICES, DEVICES, CAP), 0, A_DEV)
    paper_pos = jnp.where(corner, P_DEV - 1, paper_pos)
    author_pos = jnp.where(corner, A_DEV - 1, author_pos)
    return (live, paper_pos, author_pos)


def draw_write_dst(key, part):
    live, paper_pos, author_pos = write_common(key)
    return jnp.where(live, paper_pos, -1).astype(jnp.int32)


def draw_write_src(key, part):
    live, paper_pos, author_pos = write_common(key)
    return jnp.transpose(jnp.where(live, author_pos, -1), (1, 0, 2)).astype(jnp.int32)


def draw_cite_nbr(key, part):
    key = jax.random.fold_in(key, 11)
    keys = jax.random.split(key, 5)
    blocks = ROW_PAPERS // P_DEV
    rows = jnp.arange(PAPERS, dtype=jnp.int32)
    counts = jax.random.randint(keys[0], (PAPERS,), 0, K_CITE + 1)
    chosen = jax.random.randint(keys[1], (), 0, PAPERS)
    counts = jnp.where(rows == chosen, K_CITE, counts)
    own_block = rows // P_DEV % blocks
    stay = jax.random.randint(keys[2], (PAPERS, K_CITE), 0, 2)
    other = jax.random.randint(keys[3], (PAPERS, K_CITE), 0, blocks)
    block_id = jnp.where(stay == 0, own_block[:, None], other)
    offset = jax.random.randint(keys[4], (PAPERS, K_CITE), 0, P_DEV)
    entries = block_id * P_DEV + offset
    first = (rows[:, None] == chosen) & (jnp.arange(K_CITE, dtype=jnp.int32)[None, :] == 0)
    entries = jnp.where(first, ROW_PAPERS - 1, entries)
    valid = jnp.arange(K_CITE, dtype=jnp.int32)[None, :] < counts[:, None]
    return jnp.where(valid, entries, -1).astype(jnp.int32)


def spiked(values, own_key, source, target, shards_of, factor):
    def block_of(axis_at):
        return (jnp.arange(values.shape[axis_at]) // (values.shape[axis_at] // shards_of)).reshape((-1,) + (1,) * (values.ndim - 1 - axis_at))

    first = jax.random.permutation(own_key, shards_of)[block_of(target)]
    second = (block_of(target) + shards_of // 2) % shards_of
    return jnp.where((block_of(source) == first) | (block_of(source) == second), factor * values, values)


def steps_of(key, shape, shards, low, high):
    def one(axis_at, blocks):
        heights = jax.random.uniform(jax.random.fold_in(jax.random.fold_in(key, 6), axis_at), (blocks,), jnp.float32, low / len(shards), high / len(shards))
        return jnp.repeat(jnp.exp(heights), shape[axis_at] // blocks).reshape((-1,) + (1,) * (len(shape) - axis_at - 1))

    level = one(*shards[0])
    for cut in shards[1:]:
        level = level * one(*cut)
    return level


def normal_values(own_key, dims, width, bound, shards=(), kind=jnp.bfloat16):
    values = jax.random.normal(own_key, dims, jnp.float32) * width
    if len(shards) > 0:
        values = steps_of(own_key, dims, shards, -0.22, 0.18) * values
    return jnp.clip(values, min=-bound, max=bound).astype(kind)


def noise_with(stream_key, dims, width, limit, shards, heavy, kind=jnp.bfloat16):
    drawn = width * jax.random.normal(stream_key, dims, jnp.float32)
    if shards:
        drawn = drawn * steps_of(stream_key, dims, shards, -0.22, 0.18)
    return jnp.clip(spiked(drawn, jax.random.fold_in(stream_key, 3), *heavy), -limit, limit).astype(kind)


def setup_inputs(seed: int = 0) -> dict:
    key_of = jax.random.split(jax.random.key(seed), 13)
    return {
        "x_paper": normal_values(key_of[0], (PAPERS, D_IN), 1.0, 6.0, ((0, 32),)),
        "x_author": normal_values(key_of[1], (AUTHORS, D_IN), 1.0, 6.0, ((0, 32),)),
        "cite_nbr": draw_cite_nbr(jax.random.fold_in(key_of[12], 71), 0),
        "write_src": draw_write_src(jax.random.fold_in(key_of[12], 71), 0),
        "write_dst": draw_write_dst(jax.random.fold_in(key_of[12], 71), 0),
        "w_self_paper": normal_values(key_of[5], (D_IN, D_OUT), D_IN ** -0.5, 0.21875),
        "w_cite": normal_values(key_of[6], (D_IN, D_OUT), D_IN ** -0.5, 0.21875),
        "w_write": normal_values(key_of[7], (D_IN, D_OUT), D_IN ** -0.5, 0.21875),
        "w_self_author": normal_values(key_of[8], (D_IN, D_OUT), D_IN ** -0.5, 0.21875),
        "w_written": normal_values(key_of[9], (D_IN, D_OUT), D_IN ** -0.5, 0.21875),
        "grad_paper": noise_with(key_of[10], (PAPERS, D_OUT), 1.0, 6.0, ((0, 32),), (0, 1, 32, 2.75)),
        "grad_author": noise_with(key_of[11], (AUTHORS, D_OUT), 1.0, 6.0, ((0, 32),), (0, 1, 32, 2.75)),
    }


def authors_to_papers(values, write_src, write_dst):
    src_by_dst = jnp.transpose(write_src, (1, 0, 2))
    offsets = (jnp.arange(DEVICES, dtype=jnp.int32) * A_DEV)[:, None]

    def one_device(pair):
        src_row, dst_row = pair
        live = dst_row >= 0
        index = (offsets + jnp.maximum(src_row, 0)).reshape(-1)
        picked = values[index].astype(jnp.float32) * live.reshape(-1, 1).astype(jnp.float32)
        target = jnp.where(live, dst_row, P_DEV).reshape(-1)
        return jax.ops.segment_sum(picked, target, P_DEV + 1)[:P_DEV]

    result = lax.map(one_device, (src_by_dst, write_dst))
    return result.reshape(PAPERS, -1)


def papers_to_authors(values, write_src, write_dst):
    dst_by_src = jnp.transpose(write_dst, (1, 0, 2))
    offsets = (jnp.arange(DEVICES, dtype=jnp.int32) * P_DEV)[:, None]

    def one_device(pair):
        dst_row, src_row = pair
        live = src_row >= 0
        index = (offsets + jnp.maximum(dst_row, 0)).reshape(-1)
        picked = values[index].astype(jnp.float32) * live.reshape(-1, 1).astype(jnp.float32)
        target = jnp.where(live, src_row, A_DEV).reshape(-1)
        return jax.ops.segment_sum(picked, target, A_DEV + 1)[:A_DEV]

    result = lax.map(one_device, (dst_by_src, write_src))
    return result.reshape(AUTHORS, -1)


def cite_forward(values, cite_nbr):
    groups = values.reshape(N_ROW, ROW_PAPERS, -1)
    lists = cite_nbr.reshape(N_ROW, ROW_PAPERS, K_CITE)

    def one_group(pair):
        block, entries = pair
        live = (entries >= 0).astype(jnp.float32)
        where_from = jnp.maximum(entries, 0)
        accum = jnp.zeros((ROW_PAPERS, block.shape[1]), jnp.float32)
        for slot in range(K_CITE):
            accum = accum + block[where_from[:, slot]].astype(jnp.float32) * live[:, slot:slot + 1]
        return accum

    return lax.map(one_group, (groups, lists)).reshape(PAPERS, -1)


def cite_backward(values, cite_nbr):
    groups = values.reshape(N_ROW, ROW_PAPERS, -1)
    lists = cite_nbr.reshape(N_ROW, ROW_PAPERS, K_CITE)

    def one_group(pair):
        block, entries = pair
        live = (entries >= 0).astype(jnp.float32)
        where_to = jnp.maximum(entries, 0)
        accum = jnp.zeros((ROW_PAPERS, block.shape[1]), jnp.float32)
        for slot in range(K_CITE):
            accum = accum.at[where_to[:, slot]].add(block.astype(jnp.float32) * live[:, slot:slot + 1])
        return accum

    return lax.map(one_group, (groups, lists)).reshape(PAPERS, -1)


def silu_slope(value):
    sigma = jax.nn.sigmoid(value)
    return sigma * (1.0 + value * (1.0 - sigma))


def project_back(delta, weight):
    return jnp.dot(delta, weight.T, preferred_element_type=jnp.float32)


def contract_rows(left_side, right_side):
    return jnp.dot(left_side.T, right_side, preferred_element_type=jnp.float32)


def reference(x_paper, x_author, cite_nbr, write_src, write_dst, w_self_paper, w_cite, w_write, w_self_author, w_written, grad_paper, grad_author):
    cnt_cite = jnp.maximum(jnp.sum((cite_nbr >= 0).astype(jnp.float32), axis=1, keepdims=True), 1.0)
    cnt_write = jnp.maximum(authors_to_papers(jnp.ones((AUTHORS, 1), jnp.float32), write_src, write_dst), 1.0)
    cnt_written = jnp.maximum(papers_to_authors(jnp.ones((PAPERS, 1), jnp.float32), write_src, write_dst), 1.0)
    cited = (cite_forward(x_paper, cite_nbr) / cnt_cite).astype(jnp.bfloat16)
    written = (authors_to_papers(x_author, write_src, write_dst) / cnt_write).astype(jnp.bfloat16)
    authored = (papers_to_authors(x_paper, write_src, write_dst) / cnt_written).astype(jnp.bfloat16)
    pre_paper = (jnp.dot(x_paper, w_self_paper, preferred_element_type=jnp.float32)
                 + jnp.dot(cited, w_cite, preferred_element_type=jnp.float32)
                 + jnp.dot(written, w_write, preferred_element_type=jnp.float32))
    pre_author = (jnp.dot(x_author, w_self_author, preferred_element_type=jnp.float32)
                  + jnp.dot(authored, w_written, preferred_element_type=jnp.float32))
    out_paper = jax.nn.silu(pre_paper).astype(jnp.bfloat16)
    out_author = jax.nn.silu(pre_author).astype(jnp.bfloat16)
    dpre_paper = (grad_paper.astype(jnp.float32) * silu_slope(pre_paper)).astype(jnp.bfloat16)
    dpre_author = (grad_author.astype(jnp.float32) * silu_slope(pre_author)).astype(jnp.bfloat16)
    dz_cite = (project_back(dpre_paper, w_cite) / cnt_cite).astype(jnp.bfloat16)
    dz_write = (project_back(dpre_paper, w_write) / cnt_write).astype(jnp.bfloat16)
    dz_written = (project_back(dpre_author, w_written) / cnt_written).astype(jnp.bfloat16)
    dx_paper = (project_back(dpre_paper, w_self_paper) + cite_backward(dz_cite, cite_nbr)
                + authors_to_papers(dz_written, write_src, write_dst)).astype(jnp.bfloat16)
    dx_author = (project_back(dpre_author, w_self_author)
                 + papers_to_authors(dz_write, write_src, write_dst)).astype(jnp.bfloat16)
    paper_scale = float(PAPERS) ** -0.5
    author_scale = float(AUTHORS) ** -0.5
    dweights = jnp.stack([
        contract_rows(x_paper, dpre_paper) * paper_scale,
        contract_rows(cited, dpre_paper) * paper_scale,
        contract_rows(written, dpre_paper) * paper_scale,
        contract_rows(x_author, dpre_author) * author_scale,
        contract_rows(authored, dpre_author) * author_scale,
    ])
    return out_paper, out_author, dx_paper, dx_author, dweights
```

```python
import jax
import jax.numpy as jnp
from jax import lax
from jax.sharding import PartitionSpec as P


def match_table(entries, columns):
    accum = jnp.zeros((entries.shape[0], columns.shape[0]), jnp.float32)
    for slot in range(entries.shape[1]):
        accum = accum + (entries[:, slot : slot + 1] == columns[None, :]).astype(jnp.float32)
    return accum.astype(jnp.bfloat16)


def select_rows(values, positions):
    live = (positions >= 0)[..., None]
    picked = values[jnp.maximum(positions, 0)]
    return jnp.where(live, picked, jnp.zeros_like(picked))


def project_back(delta, weight):
    return lax.dot_general(
        delta, weight, (((1,), (1,)), ((), ())), preferred_element_type=jnp.float32
    )


def contract_rows(left_side, right_side):
    return lax.dot_general(
        left_side, right_side, (((0,), (0,)), ((), ())), preferred_element_type=jnp.float32
    )


def silu_slope(value):
    sigma = jax.nn.sigmoid(value)
    return sigma * (1.0 + value * (1.0 - sigma))


def edge_rows(from_authors, from_papers):
    stacked = jnp.stack([from_authors, from_papers])
    width = stacked.shape[-1]
    arrived = lax.all_to_all(stacked, ("row", "col"), split_axis=1, concat_axis=1, tiled=True)
    return (arrived[0].reshape(-1, width), arrived[1].reshape(-1, width))


def pick_half(value, low, high):
    return jnp.where(value == 0, low, high)


def neighbour_blocks(block):
    size = lax.axis_size("col")
    me = lax.axis_index("col")
    if size % 2:
        sources = lax.rem(me + lax.iota(jnp.int32, size), size)
        rows = lax.all_gather(block, "col", axis=0)
        return rows[sources].reshape(-1, block.shape[1]), sources
    depth = size // 2
    level = me // 2

    def across(value, valid):
        return lax.ppermute(value, "col", [(c, c ^ 1) for c in range(size) if valid(c // 2)])

    ups, downs = [block], [block]
    for hop in range(1, depth):
        ups.append(
            lax.ppermute(
                ups[-1], "col", [(c, c + 2) for c in range(size - 2) if c // 2 >= hop - 1]
            )
        )
        downs.append(
            lax.ppermute(
                downs[-1], "col", [(c, c - 2) for c in range(2, size) if c // 2 <= depth - hop]
            )
        )
    parts = [block, across(block, lambda z: True)]
    sources = [me, me ^ 1]
    ups_across = [None] + [
        across(ups[hop], lambda z, hop=hop: z >= hop) for hop in range(1, depth)
    ]
    downs_across = [None] + [
        across(downs[hop], lambda z, hop=hop: z < depth - hop) for hop in range(1, depth)
    ]
    for hop in range(1, depth):
        source = lax.rem(level - hop + depth, depth) * 2 + me % 2
        parts.append(jnp.where(level >= hop, ups[hop], downs[depth - hop]))
        parts.append(jnp.where(level >= hop, ups_across[hop], downs_across[depth - hop]))
        sources += [source, source ^ 1]
    return jnp.concatenate(parts, axis=0), jnp.stack(sources)


def swap(value, axis, bit):
    size = lax.axis_size(axis)
    return lax.ppermute(value, axis, [(i, i ^ bit) for i in range(size)])


def block_order(size):
    bits = size.bit_length() - 1
    return [sum(((i >> b) & 1) << (bits - 1 - b) for b in range(bits)) for i in range(size)]


def columns_by_lowest_bit(values):
    size = lax.axis_size("col")
    width = values.shape[1] // size
    return jnp.concatenate(
        [values[:, i * width : (i + 1) * width] for i in block_order(size)], axis=1
    )


def scatter_sum(partial, matrices):
    rows = lax.axis_size("row")
    value = partial.reshape(matrices, rows, -1, partial.shape[1])
    me = lax.axis_index("row")
    bit = 1
    while bit < rows:
        mine = (me // bit) % 2
        split = value.reshape(matrices, value.shape[1] // 2, 2, value.shape[2], value.shape[3])
        keep = lax.dynamic_index_in_dim(split, mine, 2, keepdims=False)
        send = lax.dynamic_index_in_dim(split, 1 - mine, 2, keepdims=False)
        value = keep + swap(send.astype(jnp.bfloat16), "row", bit).astype(jnp.float32)
        bit *= 2
    value = value.reshape(-1, value.shape[3])
    me = lax.axis_index("col")
    bit = 1
    while bit < lax.axis_size("col"):
        mine = (me // bit) % 2
        half = value.shape[1] // 2
        low, high = value[:, :half], value[:, half:]
        send = pick_half(mine, high, low).astype(jnp.bfloat16)
        value = pick_half(mine, low, high) + swap(send, "col", bit).astype(jnp.float32)
        bit *= 2
    return value.reshape(matrices, -1, value.shape[1])


def per_device(
    x_paper,
    x_author,
    cite_nbr,
    write_src,
    write_dst,
    w_self_paper,
    w_cite,
    w_write,
    w_self_author,
    w_written,
    grad_paper,
    grad_author,
):
    papers = x_paper.shape[0]
    authors = x_author.shape[0]
    cnt_cite = jnp.maximum(jnp.sum((cite_nbr >= 0).astype(jnp.float32), axis=1, keepdims=True), 1.0)
    rows_in, sources = neighbour_blocks(x_paper)
    positions = lax.iota(jnp.int32, papers)
    columns = (sources[:, None] * papers + positions[None, :]).reshape(-1)
    table_cite = lax.optimization_barrier(match_table(cite_nbr, columns))
    nbr_all = lax.all_gather(cite_nbr, "col", axis=0)
    nbr_here = nbr_all[sources].reshape(-1, cite_nbr.shape[1])
    table_cited = lax.optimization_barrier(
        match_table(nbr_here, lax.axis_index("col") * papers + positions)
    )
    cite_total = jnp.dot(table_cite, rows_in, preferred_element_type=jnp.float32)
    cited = (cite_total / cnt_cite).astype(jnp.bfloat16)
    send_list = write_src[0]
    take_list = write_dst[0]
    table_paper = (take_list.reshape(-1)[None, :] == lax.iota(jnp.int32, papers)[:, None]).astype(
        jnp.bfloat16
    )
    table_author = (send_list.reshape(-1)[None, :] == lax.iota(jnp.int32, authors)[:, None]).astype(
        jnp.bfloat16
    )
    cnt_write = jnp.maximum(jnp.sum(table_paper, axis=1, keepdims=True, dtype=jnp.float32), 1.0)
    cnt_written = jnp.maximum(jnp.sum(table_author, axis=1, keepdims=True, dtype=jnp.float32), 1.0)
    into_papers, into_authors = edge_rows(
        select_rows(x_author, send_list), select_rows(x_paper, take_list)
    )
    written = (
        jnp.dot(table_paper, into_papers, preferred_element_type=jnp.float32) / cnt_write
    ).astype(jnp.bfloat16)
    authored = (
        jnp.dot(table_author, into_authors, preferred_element_type=jnp.float32) / cnt_written
    ).astype(jnp.bfloat16)
    pre_paper = (
        jnp.dot(x_paper, w_self_paper, preferred_element_type=jnp.float32)
        + jnp.dot(cited, w_cite, preferred_element_type=jnp.float32)
        + jnp.dot(written, w_write, preferred_element_type=jnp.float32)
    )
    pre_author = jnp.dot(x_author, w_self_author, preferred_element_type=jnp.float32) + jnp.dot(
        authored, w_written, preferred_element_type=jnp.float32
    )
    out_paper = jax.nn.silu(pre_paper).astype(jnp.bfloat16)
    out_author = jax.nn.silu(pre_author).astype(jnp.bfloat16)
    dpre_paper = (grad_paper.astype(jnp.float32) * silu_slope(pre_paper)).astype(jnp.bfloat16)
    dpre_author = (grad_author.astype(jnp.float32) * silu_slope(pre_author)).astype(jnp.bfloat16)
    dz_cite = (project_back(dpre_paper, w_cite) / cnt_cite).astype(jnp.bfloat16)
    dz_write = (project_back(dpre_paper, w_write) / cnt_write).astype(jnp.bfloat16)
    dz_written = (project_back(dpre_author, w_written) / cnt_written).astype(jnp.bfloat16)
    dz_rows, _ = neighbour_blocks(dz_cite)
    cite_grad = contract_rows(table_cited, dz_rows)
    back_papers, back_authors = edge_rows(
        select_rows(dz_written, send_list), select_rows(dz_write, take_list)
    )
    dx_paper = (
        project_back(dpre_paper, w_self_paper)
        + cite_grad
        + jnp.dot(table_paper, back_papers, preferred_element_type=jnp.float32)
    ).astype(jnp.bfloat16)
    dx_author = (
        project_back(dpre_author, w_self_author)
        + jnp.dot(table_author, back_authors, preferred_element_type=jnp.float32)
    ).astype(jnp.bfloat16)
    turned_paper = columns_by_lowest_bit(dpre_paper)
    turned_author = columns_by_lowest_bit(dpre_author)
    author_sums = scatter_sum(
        contract_rows(jnp.concatenate([x_author, authored], axis=1), turned_author), 2
    )
    pair_sums = scatter_sum(
        contract_rows(jnp.concatenate([x_paper, written], axis=1), turned_paper), 2
    )
    cited_sum = scatter_sum(contract_rows(cited, turned_paper), 1)
    summed = jnp.concatenate([pair_sums[:1], cited_sum, pair_sums[1:], author_sums], axis=0)
    devices_all = lax.axis_size("row") * lax.axis_size("col")
    paper_scale = float(papers * devices_all) ** (-0.5)
    author_scale = float(authors * devices_all) ** (-0.5)
    factors = jnp.array(
        [paper_scale, paper_scale, paper_scale, author_scale, author_scale], jnp.float32
    )
    dweights = summed * factors[:, None, None]
    return (out_paper, out_author, dx_paper, dx_author, dweights)


def solution(mesh):
    placed = (
        P(("row", "col"), None),
        P(("row", "col"), None),
        P(("row", "col"), None),
        P(("row", "col"), None, None),
        P(("row", "col"), None, None),
        P(),
        P(),
        P(),
        P(),
        P(),
        P(("row", "col"), None),
        P(("row", "col"), None),
    )
    return jax.shard_map(
        per_device,
        mesh=mesh,
        in_specs=placed,
        out_specs=(
            P(("row", "col"), None),
            P(("row", "col"), None),
            P(("row", "col"), None),
            P(("row", "col"), None),
            P(None, "row", "col"),
        ),
        check_vma=False,
    )
```

```python
import jax
import jax.numpy as jnp
from jax import lax
from jax.experimental import pallas as pl
from jax.experimental.pallas import tpu as pltpu
from jax.sharding import PartitionSpec as P


def match_table(entries, columns):
    accum = jnp.zeros((entries.shape[0], columns.shape[0]), jnp.float32)
    for slot in range(entries.shape[1]):
        accum = accum + (entries[:, slot : slot + 1] == columns[None, :]).astype(jnp.float32)
    return accum.astype(jnp.bfloat16)


def select_rows(values, positions):
    live = (positions >= 0)[..., None]
    picked = values[jnp.maximum(positions, 0)]
    return jnp.where(live, picked, jnp.zeros_like(picked))


def project_back(delta, weight):
    return lax.dot_general(
        delta, weight, (((1,), (1,)), ((), ())), preferred_element_type=jnp.float32
    )


def contract_rows(left_side, right_side):
    return lax.dot_general(
        left_side, right_side, (((0,), (0,)), ((), ())), preferred_element_type=jnp.float32
    )


def silu_slope(value):
    sigma = jax.nn.sigmoid(value)
    return sigma * (1.0 + value * (1.0 - sigma))


def edge_rows(from_authors, from_papers):
    stacked = jnp.stack([from_authors, from_papers])
    width = stacked.shape[-1]
    arrived = lax.all_to_all(stacked, ("row", "col"), split_axis=1, concat_axis=1, tiled=True)
    return (arrived[0].reshape(-1, width), arrived[1].reshape(-1, width))


def flip(index, bit):
    return index + bit - 2 * bit * ((index // bit) % 2)


def axis_bits(axis):
    return [(axis, 1 << b) for b in range(lax.axis_size(axis).bit_length() - 1)]


class Line:
    def __init__(self, block, got, up, down, cross, landed):
        self.block, self.got, self.landed = block, got, landed
        self.up, self.down, self.cross = up, down, cross
        self.me = lax.axis_index("col")
        self.depth = lax.axis_size("col") // 2
        self.level = self.me // 2
        self.has_up = self.level + 1 < self.depth
        self.has_down = self.level > 0

    def copy(self, source, slot, target, send):
        return pltpu.make_async_remote_copy(
            src_ref=source,
            dst_ref=self.got.at[slot],
            send_sem=send.at[slot],
            recv_sem=self.landed.at[slot],
            device_id={"col": target},
            device_id_type=pl.DeviceIdType.MESH,
        )

    def go_up(self, source, slot):
        return self.copy(source, slot, self.me + 2, self.up)

    def go_down(self, source, slot):
        return self.copy(source, slot, self.me - 2, self.down)

    def go_across(self, source, slot):
        return self.copy(source, slot, flip(self.me, 1), self.cross)

    def first(self):
        @pl.when(self.has_up)
        def _():
            self.go_up(self.block, self.me).start()

        @pl.when(self.has_down)
        def _():
            self.go_down(self.block, self.me).start()

        self.go_across(self.block, self.me).start()
        self.got[self.me] = self.block[...]

    def hop(self, step):
        @pl.when(self.level >= step)
        def _():
            slot = self.me - 2 * step
            held = self.got.at[slot]
            self.go_across(held, slot).wait_recv()

            @pl.when(self.has_up)
            def _():
                self.go_up(held, slot).start()

            self.go_across(held, slot).start()

        @pl.when(self.level + step < self.depth)
        def _():
            slot = self.me + 2 * step
            held = self.got.at[slot]
            self.go_across(held, slot).wait_recv()

            @pl.when(self.has_down)
            def _():
                self.go_down(held, slot).start()

            self.go_across(held, slot).start()

    def finish(self):
        for pair in range(self.depth):
            slot = 2 * pair + 1 - self.me % 2
            self.go_across(self.got.at[slot], slot).wait_recv()
            mine = 2 * pair + self.me % 2
            self.go_across(self.block, mine).wait_send()

            @pl.when((pair <= self.level) & self.has_up)
            def _():
                self.go_up(self.block, mine).wait_send()

            @pl.when((pair >= self.level) & self.has_down)
            def _():
                self.go_down(self.block, mine).wait_send()


def greet(line, partners):
    barrier = pltpu.get_barrier_semaphore()
    for axis, bit in partners:
        pl.semaphore_signal(
            barrier,
            inc=1,
            device_id={axis: flip(lax.axis_index(axis), bit)},
            device_id_type=pl.DeviceIdType.MESH,
        )

    @pl.when(line.has_up)
    def _():
        pl.semaphore_signal(
            barrier, inc=1, device_id={"col": line.me + 2}, device_id_type=pl.DeviceIdType.MESH
        )

    @pl.when(line.has_down)
    def _():
        pl.semaphore_signal(
            barrier, inc=1, device_id={"col": line.me - 2}, device_id_type=pl.DeviceIdType.MESH
        )

    ends = line.has_up.astype(jnp.int32) + line.has_down.astype(jnp.int32)
    pl.semaphore_wait(barrier, len(partners) + ends)


def gather_kernel(block, got, up, down, cross, landed):
    line = Line(block, got, up, down, cross, landed)
    greet(line, [("col", 1)])
    line.first()
    for step in range(1, line.depth):
        line.hop(step)
    line.finish()


def line_semaphores():
    return [pltpu.SemaphoreType.DMA((lax.axis_size("col"),)) for _ in range(4)]


def gather_blocks(block):
    size = lax.axis_size("col")
    return pl.pallas_call(
        gather_kernel,
        out_shape=jax.ShapeDtypeStruct((size,) + block.shape, block.dtype),
        in_specs=[pl.BlockSpec(memory_space=pltpu.VMEM)],
        out_specs=pl.BlockSpec(memory_space=pltpu.VMEM),
        scratch_shapes=line_semaphores(),
        compiler_params=pltpu.CompilerParams(
            collective_id=0, has_side_effects=True, vmem_limit_bytes=24 * 2**20
        ),
    )(block)


def halving_counts(size):
    counts, left = [], size
    while left > 1:
        left //= 2
        counts.append(left)
    return counts


def backward_kernel(
    block, partial, got, total, up, down, cross, landed, sent, heard, acc_rows, acc, *buffers
):
    line = Line(block, got, up, down, cross, landed)
    row_stages = axis_bits("row")
    stages = row_stages + axis_bits("col")
    greet(line, stages)
    line.first()
    count = len(stages)
    send_buf, recv_buf = buffers[:count], buffers[count:]
    matrices, rows = partial.shape[:2]
    columns = lax.axis_size("col")
    width = total.shape[2]

    def copy(stage, matrix):
        axis, bit = stages[stage]
        return pltpu.make_async_remote_copy(
            src_ref=send_buf[stage].at[matrix],
            dst_ref=recv_buf[stage].at[matrix],
            send_sem=sent.at[stage, matrix],
            recv_sem=heard.at[stage, matrix],
            device_id={axis: flip(lax.axis_index(axis), bit)},
            device_id_type=pl.DeviceIdType.MESH,
        )

    mine = lax.axis_index("row") % 2

    @pl.loop(0, matrices)
    def _(matrix):
        @pl.loop(0, rows // 2)
        def _(k):
            send_buf[0][matrix, k] = partial[matrix, 2 * k + 1 - mine].astype(jnp.bfloat16)

        copy(0, matrix).start()

        @pl.loop(0, rows // 2)
        def _(k):
            acc_rows[matrix, k] = partial[matrix, 2 * k + mine]

    def add_rows(stage, matrix, keep):
        @pl.loop(0, send_buf[stage].shape[1])
        def _(n):
            at = keep(n)
            acc_rows[matrix, at] = acc_rows[matrix, at] + recv_buf[stage][matrix, n].astype(
                jnp.float32
            )

    def add_columns(stage, matrix, keep):
        @pl.loop(0, send_buf[stage].shape[1])
        def _(n):
            at = keep(n)
            acc[matrix, at] = acc[matrix, at] + recv_buf[stage][matrix, n].astype(jnp.float32)

    def split_columns(stage, matrix, keep):
        for c in range(columns):
            part = pl.ds(c * width, width)
            acc[matrix, c] = acc_rows[matrix, keep(0), :, part] + recv_buf[stage][
                matrix, 0, :, part
            ].astype(jnp.float32)

    hops = list(range(1, line.depth))
    if hops:
        line.hop(hops.pop(0))
    keep, start, step = (lambda n: n), 0, 1
    for stage in range(1, count):
        axis, bit = stages[stage]
        mine = (lax.axis_index(axis) // bit) % 2
        if stage < len(row_stages):
            add, values = add_rows, acc_rows
        elif stage == len(row_stages):
            add, values = split_columns, acc
            start, step = 0, 1
        else:
            add, values = add_columns, acc

        def place(n, side, start=start, step=step):
            return start + side * step + n * 2 * step

        @pl.loop(0, matrices)
        def _(matrix):
            copy(stage - 1, matrix).wait_recv()
            add(stage - 1, matrix, keep)

            @pl.loop(0, send_buf[stage].shape[1])
            def _(n):
                send_buf[stage][matrix, n] = values[matrix, place(n, 1 - mine)].astype(
                    jnp.bfloat16
                )

            copy(stage, matrix).start()

        keep = lambda n, place=place, mine=mine: place(n, mine)
        start, step = start + mine * step, 2 * step
        if stage == 1:
            while hops:
                line.hop(hops.pop(0))

    @pl.loop(0, matrices)
    def _(matrix):
        copy(count - 1, matrix).wait_recv()
        total[matrix] = acc[matrix, keep(0)] + recv_buf[count - 1][matrix, 0].astype(jnp.float32)
        for stage in range(count):
            copy(stage, matrix).wait_send()

    line.finish()


def gather_and_scatter(block, partial):
    rows, size = lax.axis_size("row"), lax.axis_size("col")
    matrices, depth, wide = partial.shape
    high, width = depth // rows, wide // size
    buffers = [
        pltpu.VMEM((matrices, n, high, wide), jnp.bfloat16) for n in halving_counts(rows)
    ] + [pltpu.VMEM((matrices, n, high, width), jnp.bfloat16) for n in halving_counts(size)]
    vmem = pl.BlockSpec(memory_space=pltpu.VMEM)
    return pl.pallas_call(
        backward_kernel,
        out_shape=(
            jax.ShapeDtypeStruct((size,) + block.shape, block.dtype),
            jax.ShapeDtypeStruct((matrices, high, width), jnp.float32),
        ),
        in_specs=[vmem, vmem],
        out_specs=(vmem, vmem),
        scratch_shapes=line_semaphores()
        + [pltpu.SemaphoreType.DMA((len(buffers), matrices)) for _ in range(2)]
        + [
            pltpu.VMEM((matrices, rows // 2, high, wide), jnp.float32),
            pltpu.VMEM((matrices, size, high, width), jnp.float32),
        ]
        + buffers
        + buffers,
        compiler_params=pltpu.CompilerParams(
            collective_id=1, has_side_effects=True, vmem_limit_bytes=56 * 2**20
        ),
    )(block, partial.reshape(matrices, rows, high, wide))


def listed_rows(entries, width):
    turned = entries.T
    high = jnp.floor_divide(turned, 256)
    low = turned - 256 * high
    both = jnp.concatenate([high, low], axis=1).astype(jnp.bfloat16)
    return jnp.pad(both, ((0, 0), (0, width - both.shape[1])))


def match_listed(entries, wanted):
    accum = jnp.zeros((wanted.shape[0], entries.shape[1]), jnp.float32)
    for slot in range(entries.shape[0]):
        accum = accum + (entries[slot][None, :] == wanted[:, None]).astype(jnp.float32)
    return accum.astype(jnp.bfloat16)


def per_device(
    x_paper,
    x_author,
    cite_nbr,
    write_src,
    write_dst,
    w_self_paper,
    w_cite,
    w_write,
    w_self_author,
    w_written,
    grad_paper,
    grad_author,
):
    papers = x_paper.shape[0]
    authors = x_author.shape[0]
    cnt_cite = jnp.maximum(jnp.sum((cite_nbr >= 0).astype(jnp.float32), axis=1, keepdims=True), 1.0)
    width = x_paper.shape[1]
    gathered = gather_blocks(
        jnp.concatenate([x_paper, listed_rows(cite_nbr, width)], axis=0)
    )
    rows_in = gathered[:, :papers].reshape(-1, width)
    lists = gathered[:, papers:].astype(jnp.int32)
    entries = 256 * lists[:, :, :papers] + lists[:, :, papers : 2 * papers]
    entries = jnp.transpose(entries, (1, 0, 2)).reshape(entries.shape[1], -1)
    positions = lax.iota(jnp.int32, papers)
    columns = lax.iota(jnp.int32, rows_in.shape[0])
    table_cite = match_table(cite_nbr, columns)
    table_cited = match_listed(entries, lax.axis_index("col") * papers + positions)
    cite_total = jnp.dot(table_cite, rows_in, preferred_element_type=jnp.float32)
    cited = (cite_total / cnt_cite).astype(jnp.bfloat16)
    send_list = write_src[0]
    take_list = write_dst[0]
    table_paper = (take_list.reshape(-1)[None, :] == lax.iota(jnp.int32, papers)[:, None]).astype(
        jnp.bfloat16
    )
    table_author = (send_list.reshape(-1)[None, :] == lax.iota(jnp.int32, authors)[:, None]).astype(
        jnp.bfloat16
    )
    cnt_write = jnp.maximum(jnp.sum(table_paper, axis=1, keepdims=True, dtype=jnp.float32), 1.0)
    cnt_written = jnp.maximum(jnp.sum(table_author, axis=1, keepdims=True, dtype=jnp.float32), 1.0)
    into_papers, into_authors = edge_rows(
        select_rows(x_author, send_list), select_rows(x_paper, take_list)
    )
    written = (
        jnp.dot(table_paper, into_papers, preferred_element_type=jnp.float32) / cnt_write
    ).astype(jnp.bfloat16)
    authored = (
        jnp.dot(table_author, into_authors, preferred_element_type=jnp.float32) / cnt_written
    ).astype(jnp.bfloat16)
    pre_paper = (
        jnp.dot(x_paper, w_self_paper, preferred_element_type=jnp.float32)
        + jnp.dot(cited, w_cite, preferred_element_type=jnp.float32)
        + jnp.dot(written, w_write, preferred_element_type=jnp.float32)
    )
    pre_author = jnp.dot(x_author, w_self_author, preferred_element_type=jnp.float32) + jnp.dot(
        authored, w_written, preferred_element_type=jnp.float32
    )
    out_paper = jax.nn.silu(pre_paper).astype(jnp.bfloat16)
    out_author = jax.nn.silu(pre_author).astype(jnp.bfloat16)
    dpre_paper = (grad_paper.astype(jnp.float32) * silu_slope(pre_paper)).astype(jnp.bfloat16)
    dpre_author = (grad_author.astype(jnp.float32) * silu_slope(pre_author)).astype(jnp.bfloat16)
    dz_cite = (project_back(dpre_paper, w_cite) / cnt_cite).astype(jnp.bfloat16)
    dz_write = (project_back(dpre_paper, w_write) / cnt_write).astype(jnp.bfloat16)
    dz_written = (project_back(dpre_author, w_written) / cnt_written).astype(jnp.bfloat16)
    local_grads = jnp.stack(
        [
            contract_rows(x_paper, dpre_paper),
            contract_rows(cited, dpre_paper),
            contract_rows(written, dpre_paper),
            contract_rows(x_author, dpre_author),
            contract_rows(authored, dpre_author),
        ]
    )
    dz_rows, summed = gather_and_scatter(dz_cite, local_grads)
    cite_grad = jnp.dot(
        table_cited, dz_rows.reshape(-1, width), preferred_element_type=jnp.float32
    )
    back_papers, back_authors = edge_rows(
        select_rows(dz_written, send_list), select_rows(dz_write, take_list)
    )
    dx_paper = (
        project_back(dpre_paper, w_self_paper)
        + cite_grad
        + jnp.dot(table_paper, back_papers, preferred_element_type=jnp.float32)
    ).astype(jnp.bfloat16)
    dx_author = (
        project_back(dpre_author, w_self_author)
        + jnp.dot(table_author, back_authors, preferred_element_type=jnp.float32)
    ).astype(jnp.bfloat16)
    devices_all = lax.axis_size("row") * lax.axis_size("col")
    paper_scale = float(papers * devices_all) ** (-0.5)
    author_scale = float(authors * devices_all) ** (-0.5)
    factors = jnp.array(
        [paper_scale, paper_scale, paper_scale, author_scale, author_scale], jnp.float32
    )
    dweights = summed * factors[:, None, None]
    return (out_paper, out_author, dx_paper, dx_author, dweights)


def solution(mesh):
    placed = (
        P(("row", "col"), None),
        P(("row", "col"), None),
        P(("row", "col"), None),
        P(("row", "col"), None, None),
        P(("row", "col"), None, None),
        P(),
        P(),
        P(),
        P(),
        P(),
        P(("row", "col"), None),
        P(("row", "col"), None),
    )
    return jax.shard_map(
        per_device,
        mesh=mesh,
        in_specs=placed,
        out_specs=(
            P(("row", "col"), None),
            P(("row", "col"), None),
            P(("row", "col"), None),
            P(("row", "col"), None),
            P(None, "row", "col"),
        ),
        check_vma=False,
    )
```

```python
import jax
import jax.numpy as jnp
from jax import lax
from jax.experimental import pallas as pl
from jax.experimental.pallas import tpu as pltpu
from jax.sharding import PartitionSpec as P


def select_rows(values, positions):
    live = (positions >= 0)[..., None]
    picked = values[jnp.maximum(positions, 0)]
    return jnp.where(live, picked, jnp.zeros_like(picked))


def project_back(delta, weight):
    return lax.dot_general(
        delta, weight, (((1,), (1,)), ((), ())), preferred_element_type=jnp.float32
    )


def contract_rows(left_side, right_side):
    return lax.dot_general(
        left_side, right_side, (((0,), (0,)), ((), ())), preferred_element_type=jnp.float32
    )


def silu_slope(value):
    sigma = jax.nn.sigmoid(value)
    return sigma * (1.0 + value * (1.0 - sigma))


def edge_rows(from_authors, from_papers):
    stacked = jnp.stack([from_authors, from_papers])
    width = stacked.shape[-1]
    arrived = lax.all_to_all(stacked, ("row", "col"), split_axis=1, concat_axis=1, tiled=True)
    return (arrived[0].reshape(-1, width), arrived[1].reshape(-1, width))


def flip(index, bit):
    return index + bit - 2 * bit * ((index // bit) % 2)


def axis_bits(axis):
    return [(axis, 1 << b) for b in range(lax.axis_size(axis).bit_length() - 1)]


class Line:
    def __init__(self, block, got, up, down, cross, landed):
        self.block, self.got, self.landed = block, got, landed
        self.up, self.down, self.cross = up, down, cross
        self.me = lax.axis_index("col")
        self.depth = lax.axis_size("col") // 2
        self.level = self.me // 2
        self.has_up = self.level + 1 < self.depth
        self.has_down = self.level > 0

    def copy(self, source, slot, target, send):
        return pltpu.make_async_remote_copy(
            src_ref=source,
            dst_ref=self.got.at[slot],
            send_sem=send.at[slot],
            recv_sem=self.landed.at[slot],
            device_id={"col": target},
            device_id_type=pl.DeviceIdType.MESH,
        )

    def go_up(self, source, slot):
        return self.copy(source, slot, self.me + 2, self.up)

    def go_down(self, source, slot):
        return self.copy(source, slot, self.me - 2, self.down)

    def go_across(self, source, slot):
        return self.copy(source, slot, flip(self.me, 1), self.cross)

    def first(self):
        @pl.when(self.has_up)
        def _():
            self.go_up(self.block, self.me).start()

        @pl.when(self.has_down)
        def _():
            self.go_down(self.block, self.me).start()

        self.go_across(self.block, self.me).start()
        self.got[self.me] = self.block[...]

    def hop(self, step):
        @pl.when(self.level >= step)
        def _():
            slot = self.me - 2 * step
            held = self.got.at[slot]
            self.go_across(held, slot).wait_recv()

            @pl.when(self.has_up)
            def _():
                self.go_up(held, slot).start()

            self.go_across(held, slot).start()

        @pl.when(self.level + step < self.depth)
        def _():
            slot = self.me + 2 * step
            held = self.got.at[slot]
            self.go_across(held, slot).wait_recv()

            @pl.when(self.has_down)
            def _():
                self.go_down(held, slot).start()

            self.go_across(held, slot).start()

    def finish(self):
        for pair in range(self.depth):
            slot = 2 * pair + 1 - self.me % 2
            self.go_across(self.got.at[slot], slot).wait_recv()
            mine = 2 * pair + self.me % 2
            self.go_across(self.block, mine).wait_send()

            @pl.when((pair <= self.level) & self.has_up)
            def _():
                self.go_up(self.block, mine).wait_send()

            @pl.when((pair >= self.level) & self.has_down)
            def _():
                self.go_down(self.block, mine).wait_send()


def greet(line, partners):
    barrier = pltpu.get_barrier_semaphore()
    for axis, bit in partners:
        pl.semaphore_signal(
            barrier,
            inc=1,
            device_id={axis: flip(lax.axis_index(axis), bit)},
            device_id_type=pl.DeviceIdType.MESH,
        )

    @pl.when(line.has_up)
    def _():
        pl.semaphore_signal(
            barrier, inc=1, device_id={"col": line.me + 2}, device_id_type=pl.DeviceIdType.MESH
        )

    @pl.when(line.has_down)
    def _():
        pl.semaphore_signal(
            barrier, inc=1, device_id={"col": line.me - 2}, device_id_type=pl.DeviceIdType.MESH
        )

    ends = line.has_up.astype(jnp.int32) + line.has_down.astype(jnp.int32)
    pl.semaphore_wait(barrier, len(partners) + ends)


def gather_kernel(block, entries, got, table, up, down, cross, landed):
    line = Line(block, got, up, down, cross, landed)
    greet(line, [("col", 1)])
    line.first()
    each = entries.shape[0]
    for source in range(got.shape[0]):
        wanted = source * each + lax.broadcasted_iota(jnp.int32, (each, each), 1)
        matches = jnp.zeros((each, each), jnp.float32)
        for slot in range(entries.shape[1]):
            matches += (entries[:, slot : slot + 1] == wanted).astype(jnp.float32)
        table[:, pl.ds(source * each, each)] = matches.astype(jnp.bfloat16)
        step = source + 1
        if step < line.depth:
            line.hop(step)
    line.finish()


def line_semaphores():
    return [pltpu.SemaphoreType.DMA((lax.axis_size("col"),)) for _ in range(4)]


def gather_blocks(block, entries):
    size = lax.axis_size("col")
    vmem = pl.BlockSpec(memory_space=pltpu.VMEM)
    return pl.pallas_call(
        gather_kernel,
        out_shape=(
            jax.ShapeDtypeStruct((size,) + block.shape, block.dtype),
            jax.ShapeDtypeStruct((entries.shape[0], size * entries.shape[0]), jnp.bfloat16),
        ),
        in_specs=[vmem, vmem],
        out_specs=(vmem, vmem),
        scratch_shapes=line_semaphores(),
        compiler_params=pltpu.CompilerParams(
            collective_id=0, has_side_effects=True, vmem_limit_bytes=24 * 2**20
        ),
    )(block, entries)


def halving_counts(size):
    counts, left = [], size
    while left > 1:
        left //= 2
        counts.append(left)
    return counts


def backward_kernel(
    block, left, right, entries, got, total, table, up, down, cross, landed, sent, heard, acc_rows, acc, *buffers
):
    line = Line(block, got, up, down, cross, landed)
    row_stages = axis_bits("row")
    stages = row_stages + axis_bits("col")
    greet(line, stages)
    line.first()
    count = len(stages)
    send_buf, recv_buf = buffers[:count], buffers[count:]
    matrices, rows = left.shape[:2]
    each = block.shape[0]

    def product(matrix, at):
        return jnp.dot(
            left[matrix, at], right[matrix // 3], preferred_element_type=jnp.float32
        )

    columns = lax.axis_size("col")
    width = total.shape[2]

    def copy(stage, matrix):
        axis, bit = stages[stage]
        return pltpu.make_async_remote_copy(
            src_ref=send_buf[stage].at[matrix],
            dst_ref=recv_buf[stage].at[matrix],
            send_sem=sent.at[stage, matrix],
            recv_sem=heard.at[stage, matrix],
            device_id={axis: flip(lax.axis_index(axis), bit)},
            device_id_type=pl.DeviceIdType.MESH,
        )

    mine = lax.axis_index("row") % 2

    @pl.loop(0, matrices)
    def _(matrix):
        @pl.loop(0, rows // 2)
        def _(k):
            send_buf[0][matrix, k] = product(matrix, 2 * k + 1 - mine).astype(jnp.bfloat16)

        copy(0, matrix).start()

        @pl.loop(0, rows // 2)
        def _(k):
            acc_rows[matrix, k] = product(matrix, 2 * k + mine)

    def add_rows(stage, matrix, keep):
        @pl.loop(0, send_buf[stage].shape[1])
        def _(n):
            at = keep(n)
            acc_rows[matrix, at] = acc_rows[matrix, at] + recv_buf[stage][matrix, n].astype(
                jnp.float32
            )

    def add_columns(stage, matrix, keep):
        @pl.loop(0, send_buf[stage].shape[1])
        def _(n):
            at = keep(n)
            acc[matrix, at] = acc[matrix, at] + recv_buf[stage][matrix, n].astype(jnp.float32)

    def split_columns(stage, matrix, keep):
        for c in range(columns):
            part = pl.ds(c * width, width)
            acc[matrix, c] = acc_rows[matrix, keep(0), :, part] + recv_buf[stage][
                matrix, 0, :, part
            ].astype(jnp.float32)

    hops = list(range(1, line.depth))
    if hops:
        line.hop(hops.pop(0))
    keep, start, step = (lambda n: n), 0, 1
    for stage in range(1, count):
        axis, bit = stages[stage]
        mine = (lax.axis_index(axis) // bit) % 2
        if stage < len(row_stages):
            add, values = add_rows, acc_rows
        elif stage == len(row_stages):
            add, values = split_columns, acc
            start, step = 0, 1
        else:
            add, values = add_columns, acc

        def place(n, side, start=start, step=step):
            return start + side * step + n * 2 * step

        @pl.loop(0, matrices)
        def _(matrix):
            copy(stage - 1, matrix).wait_recv()
            add(stage - 1, matrix, keep)

            @pl.loop(0, send_buf[stage].shape[1])
            def _(n):
                send_buf[stage][matrix, n] = values[matrix, place(n, 1 - mine)].astype(
                    jnp.bfloat16
                )

            copy(stage, matrix).start()

        keep = lambda n, place=place, mine=mine: place(n, mine)
        start, step = start + mine * step, 2 * step
        if stage == 1:
            wanted = line.me * each + lax.broadcasted_iota(jnp.int32, (each, each), 0)
            for source in range(columns):
                part = pl.ds(source * each, each)
                matches = jnp.zeros((each, each), jnp.float32)
                for slot in range(entries.shape[0]):
                    matches += (entries[slot : slot + 1, part] == wanted).astype(jnp.float32)
                table[:, part] = matches.astype(jnp.bfloat16)
            while hops:
                line.hop(hops.pop(0))

    @pl.loop(0, matrices)
    def _(matrix):
        copy(count - 1, matrix).wait_recv()
        total[matrix] = acc[matrix, keep(0)] + recv_buf[count - 1][matrix, 0].astype(jnp.float32)
        for stage in range(count):
            copy(stage, matrix).wait_send()

    line.finish()


def gather_and_scatter(block, left, right, entries):
    rows, size = lax.axis_size("row"), lax.axis_size("col")
    matrices, depth, each = left.shape
    wide = right.shape[2]
    high, width = depth // rows, wide // size
    buffers = [
        pltpu.VMEM((matrices, n, high, wide), jnp.bfloat16) for n in halving_counts(rows)
    ] + [pltpu.VMEM((matrices, n, high, width), jnp.bfloat16) for n in halving_counts(size)]
    vmem = pl.BlockSpec(memory_space=pltpu.VMEM)
    return pl.pallas_call(
        backward_kernel,
        out_shape=(
            jax.ShapeDtypeStruct((size,) + block.shape, block.dtype),
            jax.ShapeDtypeStruct((matrices, high, width), jnp.float32),
            jax.ShapeDtypeStruct((block.shape[0], entries.shape[1]), jnp.bfloat16),
        ),
        in_specs=[vmem] * 4,
        out_specs=(vmem,) * 3,
        scratch_shapes=line_semaphores()
        + [pltpu.SemaphoreType.DMA((len(buffers), matrices)) for _ in range(2)]
        + [
            pltpu.VMEM((matrices, rows // 2, high, wide), jnp.float32),
            pltpu.VMEM((matrices, size, high, width), jnp.float32),
        ]
        + buffers
        + buffers,
        compiler_params=pltpu.CompilerParams(
            collective_id=1, has_side_effects=True, vmem_limit_bytes=56 * 2**20
        ),
    )(block, left.reshape(matrices, rows, high, each), right, entries)


def listed_rows(entries, width):
    turned = entries.T
    high = jnp.floor_divide(turned, 256)
    low = turned - 256 * high
    both = jnp.concatenate([high, low], axis=1).astype(jnp.bfloat16)
    return jnp.pad(both, ((0, 0), (0, width - both.shape[1])))


def per_device(
    x_paper,
    x_author,
    cite_nbr,
    write_src,
    write_dst,
    w_self_paper,
    w_cite,
    w_write,
    w_self_author,
    w_written,
    grad_paper,
    grad_author,
):
    papers = x_paper.shape[0]
    authors = x_author.shape[0]
    cnt_cite = jnp.maximum(jnp.sum((cite_nbr >= 0).astype(jnp.float32), axis=1, keepdims=True), 1.0)
    width = x_paper.shape[1]
    gathered, table_cite = gather_blocks(
        jnp.concatenate([x_paper, listed_rows(cite_nbr, width)], axis=0), cite_nbr
    )
    rows_in = gathered[:, :papers].reshape(-1, width)
    lists = gathered[:, papers:].astype(jnp.int32)
    entries = 256 * lists[:, :, :papers] + lists[:, :, papers : 2 * papers]
    entries = jnp.transpose(entries, (1, 0, 2)).reshape(entries.shape[1], -1)
    cite_total = jnp.dot(table_cite, rows_in, preferred_element_type=jnp.float32)
    cited = (cite_total / cnt_cite).astype(jnp.bfloat16)
    send_list = write_src[0]
    take_list = write_dst[0]
    table_paper = (take_list.reshape(-1)[None, :] == lax.iota(jnp.int32, papers)[:, None]).astype(
        jnp.bfloat16
    )
    table_author = (send_list.reshape(-1)[None, :] == lax.iota(jnp.int32, authors)[:, None]).astype(
        jnp.bfloat16
    )
    cnt_write = jnp.maximum(jnp.sum(table_paper, axis=1, keepdims=True, dtype=jnp.float32), 1.0)
    cnt_written = jnp.maximum(jnp.sum(table_author, axis=1, keepdims=True, dtype=jnp.float32), 1.0)
    into_papers, into_authors = edge_rows(
        select_rows(x_author, send_list), select_rows(x_paper, take_list)
    )
    written = (
        jnp.dot(table_paper, into_papers, preferred_element_type=jnp.float32) / cnt_write
    ).astype(jnp.bfloat16)
    authored = (
        jnp.dot(table_author, into_authors, preferred_element_type=jnp.float32) / cnt_written
    ).astype(jnp.bfloat16)
    pre_paper = (
        jnp.dot(x_paper, w_self_paper, preferred_element_type=jnp.float32)
        + jnp.dot(cited, w_cite, preferred_element_type=jnp.float32)
        + jnp.dot(written, w_write, preferred_element_type=jnp.float32)
    )
    pre_author = jnp.dot(x_author, w_self_author, preferred_element_type=jnp.float32) + jnp.dot(
        authored, w_written, preferred_element_type=jnp.float32
    )
    out_paper = jax.nn.silu(pre_paper).astype(jnp.bfloat16)
    out_author = jax.nn.silu(pre_author).astype(jnp.bfloat16)
    dpre_paper = (grad_paper.astype(jnp.float32) * silu_slope(pre_paper)).astype(jnp.bfloat16)
    dpre_author = (grad_author.astype(jnp.float32) * silu_slope(pre_author)).astype(jnp.bfloat16)
    dz_cite = (project_back(dpre_paper, w_cite) / cnt_cite).astype(jnp.bfloat16)
    dz_write = (project_back(dpre_paper, w_write) / cnt_write).astype(jnp.bfloat16)
    dz_written = (project_back(dpre_author, w_written) / cnt_written).astype(jnp.bfloat16)
    left_sides = jnp.stack([x_paper.T, cited.T, written.T, x_author.T, authored.T])
    dz_rows, summed, table_cited = gather_and_scatter(
        dz_cite, left_sides, jnp.stack([dpre_paper, dpre_author]), entries
    )
    cite_grad = jnp.dot(
        table_cited, dz_rows.reshape(-1, width), preferred_element_type=jnp.float32
    )
    back_papers, back_authors = edge_rows(
        select_rows(dz_written, send_list), select_rows(dz_write, take_list)
    )
    dx_paper = (
        project_back(dpre_paper, w_self_paper)
        + cite_grad
        + jnp.dot(table_paper, back_papers, preferred_element_type=jnp.float32)
    ).astype(jnp.bfloat16)
    dx_author = (
        project_back(dpre_author, w_self_author)
        + jnp.dot(table_author, back_authors, preferred_element_type=jnp.float32)
    ).astype(jnp.bfloat16)
    devices_all = lax.axis_size("row") * lax.axis_size("col")
    paper_scale = float(papers * devices_all) ** (-0.5)
    author_scale = float(authors * devices_all) ** (-0.5)
    factors = jnp.array(
        [paper_scale, paper_scale, paper_scale, author_scale, author_scale], jnp.float32
    )
    dweights = summed * factors[:, None, None]
    return (out_paper, out_author, dx_paper, dx_author, dweights)


def solution(mesh):
    placed = (
        P(("row", "col"), None),
        P(("row", "col"), None),
        P(("row", "col"), None),
        P(("row", "col"), None, None),
        P(("row", "col"), None, None),
        P(),
        P(),
        P(),
        P(),
        P(),
        P(("row", "col"), None),
        P(("row", "col"), None),
    )
    return jax.shard_map(
        per_device,
        mesh=mesh,
        in_specs=placed,
        out_specs=(
            P(("row", "col"), None),
            P(("row", "col"), None),
            P(("row", "col"), None),
            P(("row", "col"), None),
            P(None, "row", "col"),
        ),
        check_vma=False,
    )
```

```python
import functools

import jax
import jax.numpy as jnp
from jax import lax
from jax.experimental import pallas as pl
from jax.experimental.pallas import tpu as pltpu
from jax.sharding import PartitionSpec as P


def select_rows(values, positions):
    live = (positions >= 0)[..., None]
    picked = values[jnp.maximum(positions, 0)]
    return jnp.where(live, picked, jnp.zeros_like(picked))


def project_back(delta, weight):
    return lax.dot_general(
        delta, weight, (((1,), (1,)), ((), ())), preferred_element_type=jnp.float32
    )


def contract_rows(left_side, right_side):
    return lax.dot_general(
        left_side, right_side, (((0,), (0,)), ((), ())), preferred_element_type=jnp.float32
    )


def silu_slope(value):
    sigma = jax.nn.sigmoid(value)
    return sigma * (1.0 + value * (1.0 - sigma))


def edge_rows(from_authors, from_papers):
    stacked = jnp.stack([from_authors, from_papers])
    width = stacked.shape[-1]
    arrived = lax.all_to_all(stacked, ("row", "col"), split_axis=1, concat_axis=1, tiled=True)
    return (arrived[0].reshape(-1, width), arrived[1].reshape(-1, width))


def flip(index, bit):
    return index + bit - 2 * bit * ((index // bit) % 2)


def axis_bits(axis):
    return [(axis, 1 << b) for b in range(lax.axis_size(axis).bit_length() - 1)]


class Line:
    def __init__(self, block, got, up, down, cross, landed):
        self.block, self.got, self.landed = block, got, landed
        self.up, self.down, self.cross = up, down, cross
        self.me = lax.axis_index("col")
        self.depth = lax.axis_size("col") // 2
        self.level = self.me // 2
        self.has_up = self.level + 1 < self.depth
        self.has_down = self.level > 0

    def copy(self, source, slot, target, send):
        return pltpu.make_async_remote_copy(
            src_ref=source,
            dst_ref=self.got.at[slot],
            send_sem=send.at[slot],
            recv_sem=self.landed.at[slot],
            device_id={"col": target},
            device_id_type=pl.DeviceIdType.MESH,
        )

    def go_up(self, source, slot):
        return self.copy(source, slot, self.me + 2, self.up)

    def go_down(self, source, slot):
        return self.copy(source, slot, self.me - 2, self.down)

    def go_across(self, source, slot):
        return self.copy(source, slot, flip(self.me, 1), self.cross)

    def first(self):
        @pl.when(self.has_up)
        def _():
            self.go_up(self.block, self.me).start()

        @pl.when(self.has_down)
        def _():
            self.go_down(self.block, self.me).start()

        self.go_across(self.block, self.me).start()
        self.got[self.me] = self.block[...]

    def hop(self, step):
        @pl.when(self.level >= step)
        def _():
            slot = self.me - 2 * step
            held = self.got.at[slot]
            self.go_across(held, slot).wait_recv()

            @pl.when(self.has_up)
            def _():
                self.go_up(held, slot).start()

            self.go_across(held, slot).start()

        @pl.when(self.level + step < self.depth)
        def _():
            slot = self.me + 2 * step
            held = self.got.at[slot]
            self.go_across(held, slot).wait_recv()

            @pl.when(self.has_down)
            def _():
                self.go_down(held, slot).start()

            self.go_across(held, slot).start()

    def finish(self):
        for pair in range(self.depth):
            slot = 2 * pair + 1 - self.me % 2
            self.go_across(self.got.at[slot], slot).wait_recv()
            mine = 2 * pair + self.me % 2
            self.go_across(self.block, mine).wait_send()

            @pl.when((pair <= self.level) & self.has_up)
            def _():
                self.go_up(self.block, mine).wait_send()

            @pl.when((pair >= self.level) & self.has_down)
            def _():
                self.go_down(self.block, mine).wait_send()


def greet(line, partners):
    barrier = pltpu.get_barrier_semaphore()
    for axis, bit in partners:
        pl.semaphore_signal(
            barrier,
            inc=1,
            device_id={axis: flip(lax.axis_index(axis), bit)},
            device_id_type=pl.DeviceIdType.MESH,
        )

    @pl.when(line.has_up)
    def _():
        pl.semaphore_signal(
            barrier, inc=1, device_id={"col": line.me + 2}, device_id_type=pl.DeviceIdType.MESH
        )

    @pl.when(line.has_down)
    def _():
        pl.semaphore_signal(
            barrier, inc=1, device_id={"col": line.me - 2}, device_id_type=pl.DeviceIdType.MESH
        )

    ends = line.has_up.astype(jnp.int32) + line.has_down.astype(jnp.int32)
    pl.semaphore_wait(barrier, len(partners) + ends)


def gather_kernel(block, entries, got, table, up, down, cross, landed):
    line = Line(block, got, up, down, cross, landed)
    greet(line, [("col", 1)])
    line.first()
    each = entries.shape[0]
    for source in range(got.shape[0]):
        wanted = source * each + lax.broadcasted_iota(jnp.int32, (each, each), 1)
        matches = jnp.zeros((each, each), jnp.float32)
        for slot in range(entries.shape[1]):
            matches += (entries[:, slot : slot + 1] == wanted).astype(jnp.float32)
        table[:, pl.ds(source * each, each)] = matches.astype(jnp.bfloat16)
        step = source + 1
        if step < line.depth:
            line.hop(step)
    line.finish()


def line_semaphores():
    return [pltpu.SemaphoreType.DMA((lax.axis_size("col"),)) for _ in range(4)]


def gather_blocks(block, entries):
    size = lax.axis_size("col")
    vmem = pl.BlockSpec(memory_space=pltpu.VMEM)
    return pl.pallas_call(
        gather_kernel,
        out_shape=(
            jax.ShapeDtypeStruct((size,) + block.shape, block.dtype),
            jax.ShapeDtypeStruct((entries.shape[0], size * entries.shape[0]), jnp.bfloat16),
        ),
        in_specs=[vmem, vmem],
        out_specs=(vmem, vmem),
        scratch_shapes=line_semaphores(),
        compiler_params=pltpu.CompilerParams(
            collective_id=0, has_side_effects=True, vmem_limit_bytes=24 * 2**20
        ),
    )(block, entries)


def halving_counts(size):
    counts, left = [], size
    while left > 1:
        left //= 2
        counts.append(left)
    return counts


def backward_kernel(matrices, block, entries, *refs):
    lefts, rights = refs[:matrices], refs[matrices : matrices + 2]
    got, total, table, up, down, cross, landed, sent, heard = refs[matrices + 2 : matrices + 11]
    acc_rows, acc, *buffers = refs[matrices + 11 :]
    line = Line(block, got, up, down, cross, landed)
    row_stages = axis_bits("row")
    stages = row_stages + axis_bits("col")
    greet(line, stages)
    line.first()
    count = len(stages)
    send_buf, recv_buf = buffers[:count], buffers[count:]
    rows = lefts[0].shape[0]
    each = block.shape[0]

    def product(matrix, at):
        return jnp.dot(
            lefts[matrix][at], rights[matrix // 3][...], preferred_element_type=jnp.float32
        )

    columns = lax.axis_size("col")
    width = total.shape[2]

    def copy(stage, matrix):
        axis, bit = stages[stage]
        return pltpu.make_async_remote_copy(
            src_ref=send_buf[stage].at[matrix],
            dst_ref=recv_buf[stage].at[matrix],
            send_sem=sent.at[stage, matrix],
            recv_sem=heard.at[stage, matrix],
            device_id={axis: flip(lax.axis_index(axis), bit)},
            device_id_type=pl.DeviceIdType.MESH,
        )

    mine = lax.axis_index("row") % 2

    for matrix in range(matrices):

        @pl.loop(0, rows // 2)
        def _(k):
            send_buf[0][matrix, k] = product(matrix, 2 * k + 1 - mine).astype(jnp.bfloat16)

        copy(0, matrix).start()

        @pl.loop(0, rows // 2)
        def _(k):
            acc_rows[matrix, k] = product(matrix, 2 * k + mine)

    def add_rows(stage, matrix, keep):
        @pl.loop(0, send_buf[stage].shape[1])
        def _(n):
            at = keep(n)
            acc_rows[matrix, at] = acc_rows[matrix, at] + recv_buf[stage][matrix, n].astype(
                jnp.float32
            )

    def add_columns(stage, matrix, keep):
        @pl.loop(0, send_buf[stage].shape[1])
        def _(n):
            at = keep(n)
            acc[matrix, at] = acc[matrix, at] + recv_buf[stage][matrix, n].astype(jnp.float32)

    def split_columns(stage, matrix, keep):
        for c in range(columns):
            part = pl.ds(c * width, width)
            acc[matrix, c] = acc_rows[matrix, keep(0), :, part] + recv_buf[stage][
                matrix, 0, :, part
            ].astype(jnp.float32)

    hops = list(range(1, line.depth))
    if hops:
        line.hop(hops.pop(0))
    keep, start, step = (lambda n: n), 0, 1
    for stage in range(1, count):
        axis, bit = stages[stage]
        mine = (lax.axis_index(axis) // bit) % 2
        if stage < len(row_stages):
            add, values = add_rows, acc_rows
        elif stage == len(row_stages):
            add, values = split_columns, acc
            start, step = 0, 1
        else:
            add, values = add_columns, acc

        def place(n, side, start=start, step=step):
            return start + side * step + n * 2 * step

        @pl.loop(0, matrices)
        def _(matrix):
            copy(stage - 1, matrix).wait_recv()
            add(stage - 1, matrix, keep)

            @pl.loop(0, send_buf[stage].shape[1])
            def _(n):
                send_buf[stage][matrix, n] = values[matrix, place(n, 1 - mine)].astype(
                    jnp.bfloat16
                )

            copy(stage, matrix).start()

        keep = lambda n, place=place, mine=mine: place(n, mine)
        start, step = start + mine * step, 2 * step
        if stage == 1:
            wanted = line.me * each + lax.broadcasted_iota(jnp.int32, (each, each), 0)
            for source in range(columns):
                part = pl.ds(source * each, each)
                matches = jnp.zeros((each, each), jnp.float32)
                for slot in range(entries.shape[0]):
                    matches += (entries[slot : slot + 1, part] == wanted).astype(jnp.float32)
                table[:, part] = matches.astype(jnp.bfloat16)
            while hops:
                line.hop(hops.pop(0))

    @pl.loop(0, matrices)
    def _(matrix):
        copy(count - 1, matrix).wait_recv()
        total[matrix] = acc[matrix, keep(0)] + recv_buf[count - 1][matrix, 0].astype(jnp.float32)
        for stage in range(count):
            copy(stage, matrix).wait_send()

    line.finish()


def gather_and_scatter(block, lefts, rights, entries):
    rows, size = lax.axis_size("row"), lax.axis_size("col")
    matrices = len(lefts)
    depth, each = lefts[0].shape
    wide = rights[0].shape[1]
    high, width = depth // rows, wide // size
    buffers = [
        pltpu.VMEM((matrices, n, high, wide), jnp.bfloat16) for n in halving_counts(rows)
    ] + [pltpu.VMEM((matrices, n, high, width), jnp.bfloat16) for n in halving_counts(size)]
    vmem = pl.BlockSpec(memory_space=pltpu.VMEM)
    return pl.pallas_call(
        functools.partial(backward_kernel, matrices),
        out_shape=(
            jax.ShapeDtypeStruct((size,) + block.shape, block.dtype),
            jax.ShapeDtypeStruct((matrices, high, width), jnp.float32),
            jax.ShapeDtypeStruct((block.shape[0], entries.shape[1]), jnp.bfloat16),
        ),
        in_specs=[vmem] * (2 + matrices + len(rights)),
        out_specs=(vmem,) * 3,
        scratch_shapes=line_semaphores()
        + [pltpu.SemaphoreType.DMA((len(buffers), matrices)) for _ in range(2)]
        + [
            pltpu.VMEM((matrices, rows // 2, high, wide), jnp.float32),
            pltpu.VMEM((matrices, size, high, width), jnp.float32),
        ]
        + buffers
        + buffers,
        compiler_params=pltpu.CompilerParams(
            collective_id=1, has_side_effects=True, vmem_limit_bytes=56 * 2**20
        ),
    )(block, entries, *[left.reshape(rows, high, each) for left in lefts], *rights)


def listed_rows(entries, width):
    turned = entries.T
    high = jnp.floor_divide(turned, 256)
    low = turned - 256 * high
    both = jnp.concatenate([high, low], axis=1).astype(jnp.bfloat16)
    return jnp.pad(both, ((0, 0), (0, width - both.shape[1])))


def per_device(
    x_paper,
    x_author,
    cite_nbr,
    write_src,
    write_dst,
    w_self_paper,
    w_cite,
    w_write,
    w_self_author,
    w_written,
    grad_paper,
    grad_author,
):
    papers = x_paper.shape[0]
    authors = x_author.shape[0]
    cnt_cite = jnp.maximum(jnp.sum((cite_nbr >= 0).astype(jnp.float32), axis=1, keepdims=True), 1.0)
    width = x_paper.shape[1]
    gathered, table_cite = gather_blocks(
        jnp.concatenate([x_paper, listed_rows(cite_nbr, width)], axis=0), cite_nbr
    )
    rows_in = gathered[:, :papers].reshape(-1, width)
    lists = gathered[:, papers:].astype(jnp.int32)
    entries = 256 * lists[:, :, :papers] + lists[:, :, papers : 2 * papers]
    entries = jnp.transpose(entries, (1, 0, 2)).reshape(entries.shape[1], -1)
    cite_total = jnp.dot(table_cite, rows_in, preferred_element_type=jnp.float32)
    cited = (cite_total / cnt_cite).astype(jnp.bfloat16)
    send_list = write_src[0]
    take_list = write_dst[0]
    table_paper = (take_list.reshape(-1)[None, :] == lax.iota(jnp.int32, papers)[:, None]).astype(
        jnp.bfloat16
    )
    table_author = (send_list.reshape(-1)[None, :] == lax.iota(jnp.int32, authors)[:, None]).astype(
        jnp.bfloat16
    )
    cnt_write = jnp.maximum(jnp.sum(table_paper, axis=1, keepdims=True, dtype=jnp.float32), 1.0)
    cnt_written = jnp.maximum(jnp.sum(table_author, axis=1, keepdims=True, dtype=jnp.float32), 1.0)
    into_papers, into_authors = edge_rows(
        select_rows(x_author, send_list), select_rows(x_paper, take_list)
    )
    written = (
        jnp.dot(table_paper, into_papers, preferred_element_type=jnp.float32) / cnt_write
    ).astype(jnp.bfloat16)
    authored = (
        jnp.dot(table_author, into_authors, preferred_element_type=jnp.float32) / cnt_written
    ).astype(jnp.bfloat16)
    pre_paper = (
        jnp.dot(x_paper, w_self_paper, preferred_element_type=jnp.float32)
        + jnp.dot(cited, w_cite, preferred_element_type=jnp.float32)
        + jnp.dot(written, w_write, preferred_element_type=jnp.float32)
    )
    pre_author = jnp.dot(x_author, w_self_author, preferred_element_type=jnp.float32) + jnp.dot(
        authored, w_written, preferred_element_type=jnp.float32
    )
    out_paper = jax.nn.silu(pre_paper).astype(jnp.bfloat16)
    out_author = jax.nn.silu(pre_author).astype(jnp.bfloat16)
    dpre_paper = (grad_paper.astype(jnp.float32) * silu_slope(pre_paper)).astype(jnp.bfloat16)
    dpre_author = (grad_author.astype(jnp.float32) * silu_slope(pre_author)).astype(jnp.bfloat16)
    dz_cite = (project_back(dpre_paper, w_cite) / cnt_cite).astype(jnp.bfloat16)
    dz_write = (project_back(dpre_paper, w_write) / cnt_write).astype(jnp.bfloat16)
    dz_written = (project_back(dpre_author, w_written) / cnt_written).astype(jnp.bfloat16)
    left_sides = [x_paper.T, cited.T, written.T, x_author.T, authored.T]
    dz_rows, summed, table_cited = gather_and_scatter(
        dz_cite, left_sides, [dpre_paper, dpre_author], entries
    )
    cite_grad = jnp.dot(
        table_cited, dz_rows.reshape(-1, width), preferred_element_type=jnp.float32
    )
    back_papers, back_authors = edge_rows(
        select_rows(dz_written, send_list), select_rows(dz_write, take_list)
    )
    dx_paper = (
        project_back(dpre_paper, w_self_paper)
        + cite_grad
        + jnp.dot(table_paper, back_papers, preferred_element_type=jnp.float32)
    ).astype(jnp.bfloat16)
    dx_author = (
        project_back(dpre_author, w_self_author)
        + jnp.dot(table_author, back_authors, preferred_element_type=jnp.float32)
    ).astype(jnp.bfloat16)
    devices_all = lax.axis_size("row") * lax.axis_size("col")
    paper_scale = float(papers * devices_all) ** (-0.5)
    author_scale = float(authors * devices_all) ** (-0.5)
    factors = jnp.array(
        [paper_scale, paper_scale, paper_scale, author_scale, author_scale], jnp.float32
    )
    dweights = summed * factors[:, None, None]
    return (out_paper, out_author, dx_paper, dx_author, dweights)


def solution(mesh):
    placed = (
        P(("row", "col"), None),
        P(("row", "col"), None),
        P(("row", "col"), None),
        P(("row", "col"), None, None),
        P(("row", "col"), None, None),
        P(),
        P(),
        P(),
        P(),
        P(),
        P(("row", "col"), None),
        P(("row", "col"), None),
    )
    return jax.shard_map(
        per_device,
        mesh=mesh,
        in_specs=placed,
        out_specs=(
            P(("row", "col"), None),
            P(("row", "col"), None),
            P(("row", "col"), None),
            P(("row", "col"), None),
            P(None, "row", "col"),
        ),
        check_vma=False,
    )
```
